128 devices in a mesh: row: 8 (over z_hi, y), col: 16 (over z_lo, x, core).
Axes of the slice: x: 4, y: 4, z: 4 (z_hi: 2, z_lo: 2; z = z_hi * 2 + z_lo), core: 2. Of those that a mesh axis runs over, the one named last changes fastest.
Arguments:
- band_vectors: float32 [65536, 4096], P(('row', 'col')), may hold values from -6 to 6
- reflectors: float32 [4, 65536, 256], P(None, 'row', 'col'), as said below
- t_factors: float32 [4, 256, 256], replicated, as said below
Outputs:
- back_vectors: float32 [65536, 4096], P('row', 'col')
The draws below stay inside these ranges and needn't reach their ends.
Inputs may be any that keep to these rules, and one draw needn't show every extreme that they name: Each column of reflectors[k] has entries of order 65536^-0.5 and no zero column. t_factors[k] is upper triangular with diagonal entries between 1.6 and 2.4.
All inputs are finite; a program needn't handle non-finite values.
Results may differ from the reference program's by a relative error of at most 0.0001.
Values sent between devices are 32-bit elements; how exact they have to be, the bound alone decides.
No kernel may reach another device: no remote copies, remote signals or barrier semaphores. Data moves between devices by JAX's collectives and lax.ppermute only.
A program may use at most 192 MiB of HBM per device.

```python
import jax
import jax.numpy as jnp
from jax import lax

N = 65536
B = 256
PANELS = 4
M = 4096


def draw_reflectors(key, part):
    key = jax.random.fold_in(key, 21)
    scale = N ** (-0.5)
    return scale * jnp.clip(jax.random.normal(key, (PANELS, N, B), jnp.float32), -6.0, 6.0)


def draw_t_factors(key, part):
    key = jax.random.fold_in(key, 11)
    diag_key = jax.random.fold_in(key, 1)
    upper_key = jax.random.fold_in(key, 2)
    spread = 0.6 * B ** (-0.5)
    upper_values = spread * jnp.clip(jax.random.normal(upper_key, (PANELS, B, B), jnp.float32), -4.0, 4.0)
    diag_values = jax.random.uniform(diag_key, (PANELS, B, B), jnp.float32, 1.6, 2.4)
    row_index = lax.broadcasted_iota(jnp.int32, (PANELS, B, B), 1)
    col_index = lax.broadcasted_iota(jnp.int32, (PANELS, B, B), 2)
    upper_part = jnp.where(col_index > row_index, upper_values, 0.0)
    diag_part = jnp.where(col_index == row_index, diag_values, 0.0)
    return upper_part + diag_part


def levels(own_key, shape, pieces, smallest, largest):
    def one(position, shards_of):
        steps = jax.random.uniform(jax.random.fold_in(jax.random.fold_in(own_key, 6), position), (shards_of,), jnp.float32, smallest / len(pieces), largest / len(pieces))
        return jnp.repeat(jnp.exp(steps), shape[position] // shards_of).reshape((-1,) + (1,) * (len(shape) - position - 1))

    factor_of = one(*pieces[0])
    for cut in pieces[1:]:
        factor_of = factor_of * one(*cut)
    return factor_of


def gaussian(key, dims, scale, bound, split=(), dtype=jnp.bfloat16):
    result = scale * jax.random.normal(key, dims, jnp.float32)
    if split:
        result = result * levels(key, dims, split, -0.22, 0.18)
    return jnp.clip(result, -bound, bound).astype(dtype)


def setup_inputs(seed: int = 0) -> dict:
    arg_keys = jax.random.split(jax.random.key(seed), 4)
    return {
        "band_vectors": gaussian(arg_keys[0], (N, M), 1.0, 6.0, ((0, 128),), jnp.float32),
        "reflectors": draw_reflectors(jax.random.fold_in(arg_keys[3], 71), 0),
        "t_factors": draw_t_factors(jax.random.fold_in(arg_keys[3], 71), 0),
    }


def reference(band_vectors, reflectors, t_factors):
    precise = lax.Precision.HIGHEST
    vectors = band_vectors
    for index in reversed(range(PANELS)):
        panel = reflectors[index]
        coeffs = jnp.dot(panel.T, vectors, precision=precise, preferred_element_type=jnp.float32)
        coeffs = jnp.dot(t_factors[index], coeffs, precision=precise, preferred_element_type=jnp.float32)
        vectors = vectors - jnp.dot(panel, coeffs, precision=precise, preferred_element_type=jnp.float32)
    return vectors
```

```python
import jax
import jax.numpy as jnp
from jax import lax
from jax.sharding import PartitionSpec as P

HIGH = lax.Precision.HIGH
HIGHEST = lax.Precision.HIGHEST


def dot(a, b, dims, precision):
    return lax.dot_general(a, b, (dims, ((), ())), precision=precision, preferred_element_type=jnp.float32)


def sum_rows(values, size):
    slices = values.reshape(size, values.shape[0] // size, values.shape[1])
    mine = lax.all_to_all(slices, "row", split_axis=0, concat_axis=0, tiled=True).sum(0)
    copies = jnp.broadcast_to(mine[None], slices.shape)
    return lax.all_to_all(copies, "row", split_axis=0, concat_axis=0, tiled=True).reshape(values.shape)


def solution(mesh):
    row_size = mesh.shape["row"]

    def local(band_vectors, reflectors, t_factors):
        count = reflectors.shape[0]
        own = jnp.swapaxes(reflectors, 1, 2)
        panels = [None] * count
        for k in reversed(range(count)):
            panels[k] = lax.all_gather(own[k], "col", axis=0, tiled=True)
        vectors = lax.all_to_all(band_vectors, "col", split_axis=1, concat_axis=0, tiled=True)
        for k in reversed(range(count)):
            sums = sum_rows(dot(panels[k], vectors, ((1,), (0,)), HIGH), row_size)
            coeffs = dot(t_factors[k], sums, ((1,), (0,)), HIGHEST)
            vectors = vectors - dot(panels[k], coeffs, ((0,), (0,)), HIGH)
        return vectors

    in_specs = (P(("row", "col"), None), P(None, "row", "col"), P())
    return jax.shard_map(local, mesh=mesh, in_specs=in_specs, out_specs=P("row", "col"), check_vma=False)
```

```python
import functools

import jax
import jax.numpy as jnp
from jax import lax
from jax.experimental import pallas as pl
from jax.experimental.pallas import tpu as pltpu
from jax.sharding import PartitionSpec as P

HIGHEST = lax.Precision.HIGHEST
TILE = 2048
VMEM = 56 * 2**20

X_SIZE = 4


def split(values):
    high = values.astype(jnp.bfloat16)
    return high, (values - high.astype(jnp.float32)).astype(jnp.bfloat16)


def three_pass(left, right, dims):
    mul = functools.partial(
        lax.dot_general, dimension_numbers=(dims, ((), ())), preferred_element_type=jnp.float32
    )
    return mul(left[0], right[0]) + (mul(left[0], right[1]) + mul(left[1], right[0]))


def read(refs):
    return jnp.concatenate([ref[...] for ref in refs], 0)


def sums_kernel(n_late, n_early, *refs):
    vectors_ref, out_ref = refs[n_late + n_early :]
    late, early = split(read(refs[:n_late])), split(read(refs[n_late : n_late + n_early]))
    vectors = split(vectors_ref[...])
    size = late[0].shape[0]
    both = tuple(jnp.concatenate([e, l], 0) for e, l in zip(early, late))

    @pl.when(pl.program_id(0) == 0)
    def _():
        out_ref[...] = jnp.zeros_like(out_ref)

    out_ref[0 : 2 * size, :] += three_pass(both, vectors, ((1,), (0,)))
    out_ref[2 * size : 3 * size, :] += three_pass(late, early, ((1,), (1,)))


def pair_sums(late, early, vectors):
    rows, columns = vectors.shape
    size = sum(part.shape[0] for part in late)
    panels = [pl.BlockSpec((part.shape[0], TILE), lambda i: (0, i)) for part in (*late, *early)]
    return pl.pallas_call(
        functools.partial(sums_kernel, len(late), len(early)),
        grid=(rows // TILE,),
        in_specs=[*panels, pl.BlockSpec((TILE, columns), lambda i: (i, 0))],
        out_specs=pl.BlockSpec((3 * size, columns), lambda i: (0, 0)),
        out_shape=jax.ShapeDtypeStruct((3 * size, columns), jnp.float32),
        compiler_params=pltpu.CompilerParams(dimension_semantics=("arbitrary",), vmem_limit_bytes=VMEM),
        cost_estimate=pl.CostEstimate(
            flops=18 * size * rows * columns,
            bytes_accessed=4 * rows * (2 * size + columns),
            transcendentals=0,
        ),
    )(*late, *early, vectors)


def update_kernel(n_late, n_early, *refs):
    coeffs_ref, vectors_ref, out_ref = refs[n_late + n_early :]
    late, early = read(refs[:n_late]), read(refs[n_late : n_late + n_early])
    size = late.shape[0]
    dims = ((0,), (0,))
    change = three_pass(split(early), split(coeffs_ref[0:size, :]), dims)
    change += three_pass(split(late), split(coeffs_ref[size : 2 * size, :]), dims)
    out_ref[...] = vectors_ref[...] - change


def pair_update(late, early, coeffs, vectors):
    rows, columns = vectors.shape
    size = sum(part.shape[0] for part in late)
    panels = [pl.BlockSpec((part.shape[0], TILE), lambda i: (0, i)) for part in (*late, *early)]
    block = pl.BlockSpec((TILE, columns), lambda i: (i, 0))
    return pl.pallas_call(
        functools.partial(update_kernel, len(late), len(early)),
        grid=(rows // TILE,),
        in_specs=[*panels, pl.BlockSpec((2 * size, columns), lambda i: (0, 0)), block],
        out_specs=block,
        out_shape=jax.ShapeDtypeStruct((rows, columns), jnp.float32),
        compiler_params=pltpu.CompilerParams(dimension_semantics=("arbitrary",), vmem_limit_bytes=VMEM),
        cost_estimate=pl.CostEstimate(
            flops=12 * size * rows * columns,
            bytes_accessed=4 * rows * (2 * size + 2 * columns),
            transcendentals=0,
        ),
    )(*late, *early, coeffs, vectors)


def sum_rows(values, size):
    slices = values.reshape(size, values.shape[0] // size, values.shape[1])
    mine = lax.all_to_all(slices, "row", split_axis=0, concat_axis=0, tiled=True).sum(0)
    copies = jnp.broadcast_to(mine[None], slices.shape)
    return lax.all_to_all(copies, "row", split_axis=0, concat_axis=0, tiled=True).reshape(values.shape)


def exact(a, b):
    return jnp.matmul(a, b, precision=HIGHEST, preferred_element_type=jnp.float32)


def step(z, core, size):
    return [(i, (i // 8 ^ z) * 8 + i // 2 % X_SIZE * 2 + (i % 2 ^ core)) for i in range(size)]


def along_x(size):
    return [[z * 8 + x * 2 + core for x in range(X_SIZE)] for z in range(size // 8) for core in range(2)]


def along_x_and_core(size):
    return [[z * 8 + rest for rest in range(8)] for z in range(size // 8)]


def one_hot(blocks, width, size):
    column = blocks[:, None] * width + jnp.arange(width)[None]
    return (column.reshape(-1, 1) == jnp.arange(size * width)[None]).astype(jnp.float32)


def orders(width, size):
    me = lax.axis_index("col")
    z, core = me // 8, me % 2
    block = jnp.arange(size)
    late = (z + block % 2) % 2 * 8 + block // 2
    early = (z + block // 4 % 2) % 2 * 8 + block % 4 * 2 + (core + block // 8) % 2
    return one_hot(late, width, size), one_hot(early, width, size)


def gather(own, size):
    def send(value, z=0, core=0):
        return lax.ppermute(value, "col", step(z, core, size))

    even, odd = own[0::2], own[1::2]
    even_z = send(even, z=1)
    odd_x = lax.all_gather(odd, "col", axis=1, tiled=True, axis_index_groups=along_x(size))
    panels = []
    for k in reversed(range(own.shape[0] // 2)):
        both = jnp.concatenate([even[k], even_z[k]], 0)
        late = lax.all_gather(both, "col", axis=0, tiled=True, axis_index_groups=along_x_and_core(size))
        near = odd_x[k]
        far = send(near, z=1)
        panels.append(((late,), (near, far, send(near, core=1), send(far, core=1))))
    return panels


def solution(mesh):
    row_size, col_size = mesh.shape["row"], mesh.shape["col"]

    def local(band_vectors, reflectors, t_factors):
        count, _, width = reflectors.shape
        own = jnp.swapaxes(reflectors, 1, 2)
        late_order, early_order = orders(width, col_size)
        vectors = lax.all_to_all(band_vectors, "col", split_axis=1, concat_axis=0, tiled=True)
        panels = gather(own, col_size)
        for first, (late, early) in zip(range(count - 2, -1, -2), panels):
            late_t = exact(exact(late_order, t_factors[first]), late_order.T)
            early_t = exact(exact(early_order, t_factors[first + 1]), early_order.T)
            size = late_t.shape[0]
            sums = sum_rows(pair_sums(late, early, vectors), row_size)
            early_coeffs = exact(early_t, sums[:size])
            rest = sums[size : 2 * size] - exact(sums[2 * size :], early_coeffs)
            coeffs = jnp.concatenate([early_coeffs, exact(late_t, rest)], 0)
            vectors = pair_update(late, early, coeffs, vectors)
        return vectors

    in_specs = (P(("row", "col"), None), P(None, "row", "col"), P())
    return jax.shard_map(local, mesh=mesh, in_specs=in_specs, out_specs=P("row", "col"), check_vma=False)
```

```python
import functools

import jax
import jax.numpy as jnp
from jax import lax
from jax.experimental import pallas as pl
from jax.experimental.pallas import tpu as pltpu
from jax.sharding import PartitionSpec as P

HIGHEST = lax.Precision.HIGHEST
TILE = 1024
DEPTH = 4
VMEM = 56 * 2**20

X_SIZE = 4


def split(values):
    high = values.astype(jnp.bfloat16)
    return high, (values - high.astype(jnp.float32)).astype(jnp.bfloat16)


def three_pass(left, right, dims):
    mul = functools.partial(
        lax.dot_general, dimension_numbers=(dims, ((), ())), preferred_element_type=jnp.float32
    )
    return mul(left[0], right[0]) + (mul(left[0], right[1]) + mul(left[1], right[0]))


def read(refs):
    return jnp.concatenate([ref[...] for ref in refs], 0)


def panel_specs(parts):
    return [buffered((part.shape[0], TILE), lambda i: (0, i)) for part in parts]


def buffered(shape, index):
    return pl.BlockSpec(shape, index, pipeline_mode=pl.Buffered(DEPTH))


def sums_kernel(n_late, n_early, *refs):
    out_ref = refs[-1]
    rows, columns = refs[-2].shape
    out_ref[...] = jnp.zeros_like(out_ref)

    def body(*tiles):
        late, early = split(read(tiles[:n_late])), split(read(tiles[n_late : n_late + n_early]))
        vectors = split(tiles[-1][...])
        size = late[0].shape[0]
        both = tuple(jnp.concatenate([e, l], 0) for e, l in zip(early, late))
        out_ref[0 : 2 * size, :] += three_pass(both, vectors, ((1,), (0,)))
        out_ref[2 * size : 3 * size, :] += three_pass(late, early, ((1,), (1,)))

    pltpu.emit_pipeline(
        body,
        grid=(rows // TILE,),
        in_specs=[*panel_specs(refs[:-2]), buffered((TILE, columns), lambda i: (i, 0))],
    )(*refs[:-1])


def pair_sums(late, early, vectors):
    rows, columns = vectors.shape
    size = sum(part.shape[0] for part in late)
    anywhere = pl.BlockSpec(memory_space=pl.ANY)
    return pl.pallas_call(
        functools.partial(sums_kernel, len(late), len(early)),
        in_specs=[anywhere] * (len(late) + len(early) + 1),
        out_specs=pl.BlockSpec(memory_space=pltpu.VMEM),
        out_shape=jax.ShapeDtypeStruct((3 * size, columns), jnp.float32),
        compiler_params=pltpu.CompilerParams(vmem_limit_bytes=VMEM),
        cost_estimate=pl.CostEstimate(
            flops=18 * size * rows * columns,
            bytes_accessed=4 * rows * (2 * size + columns),
            transcendentals=0,
        ),
    )(*late, *early, vectors)


def update_kernel(n_late, n_early, *refs):
    coeffs_ref, vectors_ref, out_ref = refs[n_late + n_early :]
    rows, columns = vectors_ref.shape
    coeffs = split(coeffs_ref[...])

    def body(*tiles):
        both = split(read((*tiles[n_late : n_late + n_early], *tiles[:n_late])))
        tiles[-1][...] = tiles[-2][...] - three_pass(both, coeffs, ((0,), (0,)))

    block = buffered((TILE, columns), lambda i: (i, 0))
    pltpu.emit_pipeline(
        body,
        grid=(rows // TILE,),
        in_specs=[*panel_specs(refs[: n_late + n_early]), block],
        out_specs=[pl.BlockSpec((TILE, columns), lambda i: (i, 0))],
    )(*refs[: n_late + n_early], vectors_ref, out_ref)


def pair_update(late, early, coeffs, vectors):
    rows, columns = vectors.shape
    size = sum(part.shape[0] for part in late)
    anywhere = pl.BlockSpec(memory_space=pl.ANY)
    return pl.pallas_call(
        functools.partial(update_kernel, len(late), len(early)),
        in_specs=[
            *[anywhere] * (len(late) + len(early)),
            pl.BlockSpec(memory_space=pltpu.VMEM),
            anywhere,
        ],
        out_specs=anywhere,
        out_shape=jax.ShapeDtypeStruct((rows, columns), jnp.float32),
        compiler_params=pltpu.CompilerParams(vmem_limit_bytes=VMEM),
        cost_estimate=pl.CostEstimate(
            flops=12 * size * rows * columns,
            bytes_accessed=4 * rows * (2 * size + 2 * columns),
            transcendentals=0,
        ),
    )(*late, *early, coeffs, vectors)


def sum_rows(values, size):
    slices = values.reshape(size, values.shape[0] // size, values.shape[1])
    mine = lax.all_to_all(slices, "row", split_axis=0, concat_axis=0, tiled=True).sum(0)
    copies = jnp.broadcast_to(mine[None], slices.shape)
    sums = lax.all_to_all(copies, "row", split_axis=0, concat_axis=0, tiled=True).reshape(values.shape)
    return sums, mine


def exact(a, b):
    return jnp.matmul(a, b, precision=HIGHEST, preferred_element_type=jnp.float32)


def step(z, x, core, size):
    return [(i, (i // 8 ^ z) * 8 + (i // 2 + x) % X_SIZE * 2 + (i % 2 ^ core)) for i in range(size)]


def send(value, z=0, x=0, core=0):
    return lax.ppermute(value, "col", step(z, x, core, lax.axis_size("col")))


def gather(value, groups):
    return lax.all_gather(value, "col", axis=value.ndim - 2, tiled=True, axis_index_groups=groups)


def along_x(size):
    return [[z * 8 + x * 2 + core for x in range(X_SIZE)] for z in range(size // 8) for core in range(2)]


def along_x_and_core(size):
    return [[z * 8 + rest for rest in range(8)] for z in range(size // 8)]


def behind(value, first):
    return lax.optimization_barrier((value, first))[0]


def reorder(factor, places):
    z, x, core = (jnp.stack([jnp.asarray(place[axis]) for place in places]) for axis in range(3))
    width = factor.shape[0] // len(places)
    column = (z % 2 * 8 + x % X_SIZE * 2 + core % 2)[:, None] * width + jnp.arange(width)[None]
    pick = (column.reshape(-1, 1) == jnp.arange(factor.shape[0])[None]).astype(jnp.float32)
    return exact(exact(pick, factor), pick.T)


def apply_pair(late, early, late_t, early_t, vectors, row_size):
    size = late_t.shape[0]
    sums, mine = sum_rows(pair_sums(late, early, vectors), row_size)
    early_coeffs = exact(early_t, sums[:size])
    rest = sums[size : 2 * size] - exact(sums[2 * size :], early_coeffs)
    coeffs = jnp.concatenate([early_coeffs, exact(late_t, rest)], 0)
    return pair_update(late, early, coeffs, vectors), mine, coeffs


def solution(mesh):
    row_size, col_size = mesh.shape["row"], mesh.shape["col"]
    cat = functools.partial(jnp.concatenate, axis=0)

    def local(band_vectors, reflectors, t_factors):
        rows, width = reflectors.shape[1:]
        own = jnp.swapaxes(reflectors, 1, 2)
        me = lax.axis_index("col")
        z, x, core = me // 8, me // 2 % X_SIZE, me % 2

        near = gather(own[3], along_x(col_size))
        blocks = band_vectors.reshape(rows // col_size, col_size, -1).transpose(1, 0, 2)
        vectors = lax.all_to_all(blocks, "col", split_axis=0, concat_axis=0, tiled=True)
        vectors = vectors.reshape(rows, -1)
        other = behind(send(own[:3], z=1), blocks)

        mine = (near, send(near, z=1))
        early = (*mine, *(send(part, core=1) for part in mine))
        early_t = reorder(
            t_factors[3],
            [(z + dz, i, core + dc) for dc in (0, 1) for dz in (0, 1) for i in range(X_SIZE)],
        )
        by_z = [(z + dz, i, c) for i in range(X_SIZE) for c in (0, 1) for dz in (0, 1)]
        late = (gather(behind(cat([own[2], other[2]]), near), along_x_and_core(col_size)),)
        late_t = reorder(t_factors[2], by_z)
        first = vectors
        vectors, slice_sum, coeffs = apply_pair(late, early, late_t, early_t, vectors, row_size)

        early = (gather(behind(cat([own[1], other[1]]), near), along_x_and_core(col_size)),)
        early_t = reorder(t_factors[1], by_z)
        two = behind(cat([own[0], other[0]]), first)
        below = behind(send(two, x=1), slice_sum)
        above = behind(send(two, x=-1), slice_sum)
        across = send(below[:width], x=1), send(above[width:], x=-1)
        mine = behind(cat([two, below, above, *across]), coeffs)
        late = (mine, send(mine, core=1))
        late_t = reorder(
            t_factors[0],
            [(z + dz, x + dx, core + dc) for dc in (0, 1) for dx in (0, -1, 1, 2) for dz in (0, 1)],
        )
        vectors, _, _ = apply_pair(late, early, late_t, early_t, vectors, row_size)
        return vectors

    in_specs = (P(("row", "col"), None), P(None, "row", "col"), P())
    return jax.shard_map(local, mesh=mesh, in_specs=in_specs, out_specs=P("row", "col"), check_vma=False)
```

```python
import functools

import jax
import jax.numpy as jnp
from jax import lax
from jax.experimental import pallas as pl
from jax.experimental.pallas import tpu as pltpu
from jax.sharding import PartitionSpec as P

HIGHEST = lax.Precision.HIGHEST
TILE = 1024
DEPTH = 4
VMEM = 56 * 2**20

X_SIZE = 4


def split(values):
    high = values.astype(jnp.bfloat16)
    return high, (values - high.astype(jnp.float32)).astype(jnp.bfloat16)


def three_pass(left, right, dims):
    mul = functools.partial(
        lax.dot_general, dimension_numbers=(dims, ((), ())), preferred_element_type=jnp.float32
    )
    return mul(left[0], right[0]) + (mul(left[0], right[1]) + mul(left[1], right[0]))


def read(refs):
    return jnp.concatenate([ref[...] for ref in refs], 0)


def panel_specs(parts):
    return [buffered((part.shape[0], TILE), lambda i: (0, i)) for part in parts]


def buffered(shape, index):
    return pl.BlockSpec(shape, index, pipeline_mode=pl.Buffered(DEPTH))


def views(refs, parts):
    return [ref if index is None else ref.at[index] for ref, (_, index) in zip(refs, parts)]


def arrays(parts):
    return [array for array, _ in parts]


def shapes(parts):
    return tuple((array.shape, index) for array, index in parts)


def height(parts):
    return sum(array.shape[-2] for array, _ in parts)


def sums_kernel(late, early, *refs):
    n_late, n_early = len(late), len(early)
    out_ref = refs[-1]
    panels = views(refs, late + early)
    rows, columns = refs[-2].shape
    out_ref[...] = jnp.zeros_like(out_ref)

    def body(*tiles):
        late, early = split(read(tiles[:n_late])), split(read(tiles[n_late : n_late + n_early]))
        vectors = split(tiles[-1][...])
        size = late[0].shape[0]
        both = tuple(jnp.concatenate([e, l], 0) for e, l in zip(early, late))
        out_ref[0 : 2 * size, :] += three_pass(both, vectors, ((1,), (0,)))
        out_ref[2 * size : 3 * size, :] += three_pass(late, early, ((1,), (1,)))

    pltpu.emit_pipeline(
        body,
        grid=(rows // TILE,),
        in_specs=[*panel_specs(panels), buffered((TILE, columns), lambda i: (i, 0))],
    )(*panels, refs[-2])


def pair_sums(late, early, vectors):
    rows, columns = vectors.shape
    size = height(late)
    anywhere = pl.BlockSpec(memory_space=pl.ANY)
    return pl.pallas_call(
        functools.partial(sums_kernel, shapes(late), shapes(early)),
        in_specs=[anywhere] * (len(late) + len(early) + 1),
        out_specs=pl.BlockSpec(memory_space=pltpu.VMEM),
        out_shape=jax.ShapeDtypeStruct((3 * size, columns), jnp.float32),
        compiler_params=pltpu.CompilerParams(vmem_limit_bytes=VMEM),
        cost_estimate=pl.CostEstimate(
            flops=18 * size * rows * columns,
            bytes_accessed=4 * rows * (2 * size + columns),
            transcendentals=0,
        ),
    )(*arrays(late + early), vectors)


def update_kernel(late, early, *refs):
    n_late, n_early = len(late), len(early)
    panels = views(refs, late + early)
    coeffs_ref, vectors_ref, out_ref = refs[n_late + n_early :]
    rows, columns = vectors_ref.shape
    coeffs = split(coeffs_ref[...])

    def body(*tiles):
        both = split(read((*tiles[n_late : n_late + n_early], *tiles[:n_late])))
        tiles[-1][...] = tiles[-2][...] - three_pass(both, coeffs, ((0,), (0,)))

    block = buffered((TILE, columns), lambda i: (i, 0))
    pltpu.emit_pipeline(
        body,
        grid=(rows // TILE,),
        in_specs=[*panel_specs(panels), block],
        out_specs=[pl.BlockSpec((TILE, columns), lambda i: (i, 0))],
    )(*panels, vectors_ref, out_ref)


def pair_update(late, early, coeffs, vectors):
    rows, columns = vectors.shape
    size = height(late)
    anywhere = pl.BlockSpec(memory_space=pl.ANY)
    return pl.pallas_call(
        functools.partial(update_kernel, shapes(late), shapes(early)),
        in_specs=[
            *[anywhere] * (len(late) + len(early)),
            pl.BlockSpec(memory_space=pltpu.VMEM),
            anywhere,
        ],
        out_specs=anywhere,
        out_shape=jax.ShapeDtypeStruct((rows, columns), jnp.float32),
        compiler_params=pltpu.CompilerParams(vmem_limit_bytes=VMEM),
        cost_estimate=pl.CostEstimate(
            flops=12 * size * rows * columns,
            bytes_accessed=4 * rows * (2 * size + 2 * columns),
            transcendentals=0,
        ),
    )(*arrays(late + early), coeffs, vectors)


def sum_rows(values, size):
    slices = values.reshape(size, values.shape[0] // size, values.shape[1])
    mine = lax.all_to_all(slices, "row", split_axis=0, concat_axis=0, tiled=True).sum(0)
    copies = jnp.broadcast_to(mine[None], slices.shape)
    return lax.all_to_all(copies, "row", split_axis=0, concat_axis=0, tiled=True).reshape(values.shape)


def exact(a, b):
    return jnp.matmul(a, b, precision=HIGHEST, preferred_element_type=jnp.float32)


def step(z, x, core, size):
    return [(i, (i // 8 ^ z) * 8 + (i // 2 + x) % X_SIZE * 2 + (i % 2 ^ core)) for i in range(size)]


def send(value, z=0, x=0, core=0):
    return lax.ppermute(value, "col", step(z, x, core, lax.axis_size("col")))


def gather(value, groups):
    return lax.all_gather(value, "col", axis=value.ndim - 2, tiled=True, axis_index_groups=groups)


def along_x_and_core(size):
    return [[z * 8 + rest for rest in range(8)] for z in range(size // 8)]


def behind(value, first):
    return lax.optimization_barrier((value, first))[0]


def reorder(factor, places):
    z, x, core = (jnp.stack([jnp.asarray(place[axis]) for place in places]) for axis in range(3))
    width = factor.shape[0] // len(places)
    column = (z % 2 * 8 + x % X_SIZE * 2 + core % 2)[:, None] * width + jnp.arange(width)[None]
    pick = (column.reshape(-1, 1) == jnp.arange(factor.shape[0])[None]).astype(jnp.float32)
    return exact(exact(pick, factor), pick.T)


def apply_pair(late, early, late_t, early_t, vectors, row_size):
    size = late_t.shape[0]
    sums = sum_rows(pair_sums(late, early, vectors), row_size)
    early_coeffs = exact(early_t, sums[:size])
    rest = sums[size : 2 * size] - exact(sums[2 * size :], early_coeffs)
    coeffs = jnp.concatenate([early_coeffs, exact(late_t, rest)], 0)
    return pair_update(late, early, coeffs, vectors)


def solution(mesh):
    row_size, col_size = mesh.shape["row"], mesh.shape["col"]
    cat = functools.partial(jnp.concatenate, axis=0)

    def local(band_vectors, reflectors, t_factors):
        rows, width = reflectors.shape[1:]
        own = jnp.swapaxes(reflectors, 1, 2)
        me = lax.axis_index("col")
        z, x, core = me // 8, me // 2 % X_SIZE, me % 2

        near = gather(own[3], along_x_and_core(col_size))
        blocks = band_vectors.reshape(rows // col_size, col_size, -1).transpose(1, 0, 2)
        vectors = lax.all_to_all(blocks, "col", split_axis=0, concat_axis=0, tiled=True)
        vectors = vectors.reshape(rows, -1)
        other = behind(send(own[:3], z=1), blocks)

        blocks_x = near.reshape(X_SIZE, 2, width, rows)
        far = send(lax.dynamic_index_in_dim(blocks_x, core, 1, False).reshape(-1, rows), z=1)
        early = ((near, None), (far, None), (send(far, core=1), None))
        early_t = reorder(
            t_factors[3],
            [(z, i, c) for i in range(X_SIZE) for c in (0, 1)]
            + [(z + 1, i, core + dc) for dc in (0, 1) for i in range(X_SIZE)],
        )
        late = ((gather(behind(cat([own[2], other[2]]), near), along_x_and_core(col_size)), None),)
        by_z = [(z + dz, i, c) for i in range(X_SIZE) for c in (0, 1) for dz in (0, 1)]
        late_t = reorder(t_factors[2], by_z)
        vectors = apply_pair(late, early, late_t, early_t, vectors, row_size)

        both = jnp.concatenate([own[:2], other[:2]], 1)
        panels = gather(behind(both, near), along_x_and_core(col_size))
        late_t, early_t = reorder(t_factors[0], by_z), reorder(t_factors[1], by_z)
        return apply_pair(((panels, 0),), ((panels, 1),), late_t, early_t, vectors, row_size)

    in_specs = (P(("row", "col"), None), P(None, "row", "col"), P())
    return jax.shard_map(local, mesh=mesh, in_specs=in_specs, out_specs=P("row", "col"), check_vma=False)
```

```python
import functools

import jax
import jax.numpy as jnp
from jax import lax
from jax.experimental import pallas as pl
from jax.experimental.pallas import tpu as pltpu
from jax.sharding import PartitionSpec as P

HIGHEST = lax.Precision.HIGHEST
TILE = 1024
DEPTH = 4
VMEM = 50 * 2**20

X_SIZE = 4


def split(values):
    high = values.astype(jnp.bfloat16)
    return high, (values - high.astype(jnp.float32)).astype(jnp.bfloat16)


def three_pass(left, right, dims):
    mul = functools.partial(
        lax.dot_general, dimension_numbers=(dims, ((), ())), preferred_element_type=jnp.float32
    )
    return mul(left[0], right[0]) + (mul(left[0], right[1]) + mul(left[1], right[0]))


def read(refs):
    return jnp.concatenate([ref[...] for ref in refs], 0)


def panel_specs(parts):
    return [buffered((part.shape[0], TILE), lambda i: (0, i)) for part in parts]


def buffered(shape, index):
    return pl.BlockSpec(shape, index, pipeline_mode=pl.Buffered(DEPTH))


def views(refs, parts):
    return [ref if index is None else ref.at[index] for ref, (_, index) in zip(refs, parts)]


def arrays(parts):
    return [array for array, _ in parts]


def shapes(parts):
    return tuple((array.shape, index) for array, index in parts)


def height(parts):
    return sum(array.shape[-2] for array, _ in parts)


def sums_kernel(late, early, *refs):
    n_late, n_early = len(late), len(early)
    out_ref = refs[-1]
    panels = views(refs, late + early)
    rows, columns = refs[-2].shape
    out_ref[...] = jnp.zeros_like(out_ref)

    def body(*tiles):
        late, early = split(read(tiles[:n_late])), split(read(tiles[n_late : n_late + n_early]))
        vectors = split(tiles[-1][...])
        size = late[0].shape[0]
        both = tuple(jnp.concatenate([e, l], 0) for e, l in zip(early, late))
        out_ref[0 : 2 * size, :] += three_pass(both, vectors, ((1,), (0,)))
        out_ref[2 * size : 3 * size, :] += three_pass(late, early, ((1,), (1,)))

    pltpu.emit_pipeline(
        body,
        grid=(rows // TILE,),
        in_specs=[*panel_specs(panels), buffered((TILE, columns), lambda i: (i, 0))],
    )(*panels, refs[-2])


def pair_sums(late, early, vectors):
    rows, columns = vectors.shape
    size = height(late)
    anywhere = pl.BlockSpec(memory_space=pl.ANY)
    return pl.pallas_call(
        functools.partial(sums_kernel, shapes(late), shapes(early)),
        in_specs=[anywhere] * (len(late) + len(early) + 1),
        out_specs=pl.BlockSpec(memory_space=pltpu.VMEM),
        out_shape=jax.ShapeDtypeStruct((3 * size, columns), jnp.float32),
        compiler_params=pltpu.CompilerParams(vmem_limit_bytes=VMEM),
        cost_estimate=pl.CostEstimate(
            flops=18 * size * rows * columns,
            bytes_accessed=4 * rows * (2 * size + columns),
            transcendentals=0,
        ),
    )(*arrays(late + early), vectors)


def update_kernel(late, early, *refs):
    n_late, n_early = len(late), len(early)
    panels = views(refs, late + early)
    coeffs_ref, vectors_ref, out_ref = refs[n_late + n_early :]
    rows, columns = vectors_ref.shape
    coeffs = split(coeffs_ref[...])

    def body(*tiles):
        both = split(read((*tiles[n_late : n_late + n_early], *tiles[:n_late])))
        tiles[-1][...] = tiles[-2][...] - three_pass(both, coeffs, ((0,), (0,)))

    block = buffered((TILE, columns), lambda i: (i, 0))
    pltpu.emit_pipeline(
        body,
        grid=(rows // TILE,),
        in_specs=[*panel_specs(panels), block],
        out_specs=[pl.BlockSpec((TILE, columns), lambda i: (i, 0))],
    )(*panels, vectors_ref, out_ref)


def pair_update(late, early, coeffs, vectors):
    rows, columns = vectors.shape
    size = height(late)
    anywhere = pl.BlockSpec(memory_space=pl.ANY)
    return pl.pallas_call(
        functools.partial(update_kernel, shapes(late), shapes(early)),
        in_specs=[
            *[anywhere] * (len(late) + len(early)),
            pl.BlockSpec(memory_space=pltpu.VMEM),
            anywhere,
        ],
        out_specs=anywhere,
        out_shape=jax.ShapeDtypeStruct((rows, columns), jnp.float32),
        compiler_params=pltpu.CompilerParams(vmem_limit_bytes=VMEM),
        cost_estimate=pl.CostEstimate(
            flops=12 * size * rows * columns,
            bytes_accessed=4 * rows * (2 * size + 2 * columns),
            transcendentals=0,
        ),
    )(*arrays(late + early), coeffs, vectors)


def sum_rows(values, size):
    slices = values.reshape(size, values.shape[0] // size, values.shape[1])
    mine = lax.all_to_all(slices, "row", split_axis=0, concat_axis=0, tiled=True).sum(0)
    copies = jnp.broadcast_to(mine[None], slices.shape)
    return lax.all_to_all(copies, "row", split_axis=0, concat_axis=0, tiled=True).reshape(values.shape)


def exact(a, b):
    return jnp.matmul(a, b, precision=HIGHEST, preferred_element_type=jnp.float32)


def step(z, x, core, size):
    return [(i, (i // 8 ^ z) * 8 + (i // 2 + x) % X_SIZE * 2 + (i % 2 ^ core)) for i in range(size)]


def send(value, z=0, x=0, core=0):
    return lax.ppermute(value, "col", step(z, x, core, lax.axis_size("col")))


def gather(value, groups):
    return lax.all_gather(value, "col", axis=value.ndim - 2, tiled=True, axis_index_groups=groups)


def along_x_and_core(size):
    return [[z * 8 + rest for rest in range(8)] for z in range(size // 8)]


def behind(value, first):
    return lax.optimization_barrier((value, first))[0]


def reorder(factor, places):
    z, x, core = (jnp.stack([jnp.asarray(place[axis]) for place in places]) for axis in range(3))
    width = factor.shape[0] // len(places)
    column = (z % 2 * 8 + x % X_SIZE * 2 + core % 2)[:, None] * width + jnp.arange(width)[None]
    pick = (column.reshape(-1, 1) == jnp.arange(factor.shape[0])[None]).astype(jnp.float32)
    return exact(exact(pick, factor), pick.T)


def apply_pair(late, early, late_t, early_t, vectors, row_size):
    size = late_t.shape[0]
    sums = sum_rows(pair_sums(late, early, vectors), row_size)
    early_coeffs = exact(early_t, sums[:size])
    rest = sums[size : 2 * size] - exact(sums[2 * size :], early_coeffs)
    coeffs = jnp.concatenate([early_coeffs, exact(late_t, rest)], 0)
    return pair_update(late, early, coeffs, vectors)


def solution(mesh):
    row_size, col_size = mesh.shape["row"], mesh.shape["col"]
    cat = functools.partial(jnp.concatenate, axis=0)

    def local(band_vectors, reflectors, t_factors):
        rows, width = reflectors.shape[1:]
        own = jnp.swapaxes(reflectors, 1, 2)
        me = lax.axis_index("col")
        z, x, core = me // 8, me // 2 % X_SIZE, me % 2

        near = gather(own[3], along_x_and_core(col_size))
        blocks = band_vectors.reshape(rows // col_size, col_size, -1).transpose(1, 0, 2)
        vectors = lax.all_to_all(blocks, "col", split_axis=0, concat_axis=0, tiled=True)
        vectors = vectors.reshape(rows, -1)
        other = behind(send(own[:3], z=1), blocks)

        blocks_x = near.reshape(X_SIZE, 2, width, rows)
        far = send(lax.dynamic_index_in_dim(blocks_x, core, 1, False).reshape(-1, rows), z=1)
        early = ((near, None), (far, None), (send(far, core=1), None))
        early_t = reorder(
            t_factors[3],
            [(z, i, c) for i in range(X_SIZE) for c in (0, 1)]
            + [(z + 1, i, core + dc) for dc in (0, 1) for i in range(X_SIZE)],
        )
        late = ((gather(behind(cat([own[2], other[2]]), near), along_x_and_core(col_size)), None),)
        by_z = [(z + dz, i, c) for i in range(X_SIZE) for c in (0, 1) for dz in (0, 1)]
        late_t = reorder(t_factors[2], by_z)
        vectors = apply_pair(late, early, late_t, early_t, vectors, row_size)

        both = jnp.concatenate([own[:2], other[:2]], 1)
        panels = gather(behind(both, near), along_x_and_core(col_size))
        late_t, early_t = reorder(t_factors[0], by_z), reorder(t_factors[1], by_z)
        return apply_pair(((panels, 0),), ((panels, 1),), late_t, early_t, vectors, row_size)

    in_specs = (P(("row", "col"), None), P(None, "row", "col"), P())
    return jax.shard_map(local, mesh=mesh, in_specs=in_specs, out_specs=P("row", "col"), check_vma=False)
```

```python
import functools

import jax
import jax.numpy as jnp
from jax import lax
from jax.experimental import pallas as pl
from jax.experimental.pallas import tpu as pltpu
from jax.sharding import PartitionSpec as P

HIGHEST = lax.Precision.HIGHEST
TILE = 1024
DEPTH = 4
VMEM = 50 * 2**20

X_SIZE = 4


def split(values):
    high = values.astype(jnp.bfloat16)
    return high, (values - high.astype(jnp.float32)).astype(jnp.bfloat16)


def three_pass(left, right, dims):
    mul = functools.partial(
        lax.dot_general, dimension_numbers=(dims, ((), ())), preferred_element_type=jnp.float32
    )
    return mul(left[0], right[0]) + (mul(left[0], right[1]) + mul(left[1], right[0]))


def read(refs):
    return jnp.concatenate([ref[...] for ref in refs], 0)


def panel_specs(parts):
    return [buffered((part.shape[0], TILE), lambda i: (0, i)) for part in parts]


def buffered(shape, index):
    return pl.BlockSpec(shape, index, pipeline_mode=pl.Buffered(DEPTH))


def views(refs, parts):
    return [ref if index is None else ref.at[index] for ref, (_, index) in zip(refs, parts)]


def arrays(parts):
    return [array for array, _ in parts]


def shapes(parts):
    return tuple((array.shape, index) for array, index in parts)


def height(parts):
    return sum(array.shape[-2] for array, _ in parts)


def sums_kernel(late, early, *refs):
    n_late, n_early = len(late), len(early)
    out_ref = refs[-1]
    panels = views(refs, late + early)
    rows, columns = refs[-2].shape
    out_ref[...] = jnp.zeros_like(out_ref)

    def body(*tiles):
        late, early = split(read(tiles[:n_late])), split(read(tiles[n_late : n_late + n_early]))
        vectors = split(tiles[-1][...])
        size = late[0].shape[0]
        both = tuple(jnp.concatenate([e, l], 0) for e, l in zip(early, late))
        out_ref[0 : 2 * size, :] += three_pass(both, vectors, ((1,), (0,)))
        out_ref[2 * size : 3 * size, :] += three_pass(late, early, ((1,), (1,)))

    pltpu.emit_pipeline(
        body,
        grid=(rows // TILE,),
        in_specs=[*panel_specs(panels), buffered((TILE, columns), lambda i: (i, 0))],
    )(*panels, refs[-2])


def pair_sums(late, early, vectors):
    rows, columns = vectors.shape
    size = height(late)
    anywhere = pl.BlockSpec(memory_space=pl.ANY)
    return pl.pallas_call(
        functools.partial(sums_kernel, shapes(late), shapes(early)),
        in_specs=[anywhere] * (len(late) + len(early) + 1),
        out_specs=pl.BlockSpec(memory_space=pltpu.VMEM),
        out_shape=jax.ShapeDtypeStruct((3 * size, columns), jnp.float32),
        compiler_params=pltpu.CompilerParams(vmem_limit_bytes=VMEM),
        cost_estimate=pl.CostEstimate(
            flops=18 * size * rows * columns,
            bytes_accessed=4 * rows * (2 * size + columns),
            transcendentals=0,
        ),
    )(*arrays(late + early), vectors)


def update_kernel(late, early, *refs):
    n_late, n_early = len(late), len(early)
    count = n_late + n_early
    panels = views(refs, late + early)
    sums_ref, late_t_ref, early_t_ref, vectors_ref, out_ref, high_ref, low_ref = refs[count:]
    rows, columns = vectors_ref.shape
    size = late_t_ref.shape[0]

    def body(*tiles):
        @pl.when(pl.program_id(0) == 0)
        def _():
            early_coeffs = exact(early_t_ref[...], sums_ref[0:size, :])
            rest = sums_ref[size : 2 * size, :] - exact(sums_ref[2 * size : 3 * size, :], early_coeffs)
            high, low = split(jnp.concatenate([early_coeffs, exact(late_t_ref[...], rest)], 0))
            high_ref[...] = high
            low_ref[...] = low

        both = split(read((*tiles[n_late:count], *tiles[:n_late])))
        change = three_pass(both, (high_ref[...], low_ref[...]), ((0,), (0,)))
        tiles[-1][...] = tiles[-2][...] - change

    block = buffered((TILE, columns), lambda i: (i, 0))
    pltpu.emit_pipeline(
        body,
        grid=(rows // TILE,),
        in_specs=[*panel_specs(panels), block],
        out_specs=[pl.BlockSpec((TILE, columns), lambda i: (i, 0))],
    )(*panels, vectors_ref, out_ref)


def pair_update(late, early, sums, late_t, early_t, vectors):
    rows, columns = vectors.shape
    size = height(late)
    anywhere = pl.BlockSpec(memory_space=pl.ANY)
    vmem = pl.BlockSpec(memory_space=pltpu.VMEM)
    return pl.pallas_call(
        functools.partial(update_kernel, shapes(late), shapes(early)),
        in_specs=[*[anywhere] * (len(late) + len(early)), vmem, vmem, vmem, anywhere],
        out_specs=anywhere,
        out_shape=jax.ShapeDtypeStruct((rows, columns), jnp.float32),
        scratch_shapes=[pltpu.VMEM((2 * size, columns), jnp.bfloat16)] * 2,
        compiler_params=pltpu.CompilerParams(vmem_limit_bytes=VMEM),
        cost_estimate=pl.CostEstimate(
            flops=12 * size * rows * columns,
            bytes_accessed=4 * rows * (2 * size + 2 * columns),
            transcendentals=0,
        ),
    )(*arrays(late + early), sums, late_t, early_t, vectors)


def sum_rows(values, size):
    slices = values.reshape(size, values.shape[0] // size, values.shape[1])
    mine = lax.all_to_all(slices, "row", split_axis=0, concat_axis=0, tiled=True).sum(0)
    copies = jnp.broadcast_to(mine[None], slices.shape)
    return lax.all_to_all(copies, "row", split_axis=0, concat_axis=0, tiled=True).reshape(values.shape)


def exact(a, b):
    return jnp.matmul(a, b, precision=HIGHEST, preferred_element_type=jnp.float32)


def step(z, x, core, size):
    return [(i, (i // 8 ^ z) * 8 + (i // 2 + x) % X_SIZE * 2 + (i % 2 ^ core)) for i in range(size)]


def send(value, z=0, x=0, core=0):
    return lax.ppermute(value, "col", step(z, x, core, lax.axis_size("col")))


def gather(value, groups):
    return lax.all_gather(value, "col", axis=value.ndim - 2, tiled=True, axis_index_groups=groups)


def along_x_and_core(size):
    return [[z * 8 + rest for rest in range(8)] for z in range(size // 8)]


def behind(value, first):
    return lax.optimization_barrier((value, first))[0]


def reorder(factor, places):
    z, x, core = (jnp.stack([jnp.asarray(place[axis]) for place in places]) for axis in range(3))
    width = factor.shape[0] // len(places)
    column = (z % 2 * 8 + x % X_SIZE * 2 + core % 2)[:, None] * width + jnp.arange(width)[None]
    pick = (column.reshape(-1, 1) == jnp.arange(factor.shape[0])[None]).astype(jnp.float32)
    return exact(exact(pick, factor), pick.T)


def apply_pair(late, early, late_t, early_t, vectors, row_size):
    sums = sum_rows(pair_sums(late, early, vectors), row_size)
    return pair_update(late, early, sums, late_t, early_t, vectors)


def solution(mesh):
    row_size, col_size = mesh.shape["row"], mesh.shape["col"]
    cat = functools.partial(jnp.concatenate, axis=0)

    def local(band_vectors, reflectors, t_factors):
        rows, width = reflectors.shape[1:]
        own = jnp.swapaxes(reflectors, 1, 2)
        me = lax.axis_index("col")
        z, x, core = me // 8, me // 2 % X_SIZE, me % 2

        near = gather(own[3], along_x_and_core(col_size))
        blocks = band_vectors.reshape(rows // col_size, col_size, -1).transpose(1, 0, 2)
        vectors = lax.all_to_all(blocks, "col", split_axis=0, concat_axis=0, tiled=True)
        vectors = vectors.reshape(rows, -1)
        other = behind(send(own[:3], z=1), blocks)

        blocks_x = near.reshape(X_SIZE, 2, width, rows)
        far = send(lax.dynamic_index_in_dim(blocks_x, core, 1, False).reshape(-1, rows), z=1)
        early = ((near, None), (far, None), (send(far, core=1), None))
        early_t = reorder(
            t_factors[3],
            [(z, i, c) for i in range(X_SIZE) for c in (0, 1)]
            + [(z + 1, i, core + dc) for dc in (0, 1) for i in range(X_SIZE)],
        )
        late = ((gather(behind(cat([own[2], other[2]]), near), along_x_and_core(col_size)), None),)
        by_z = [(z + dz, i, c) for i in range(X_SIZE) for c in (0, 1) for dz in (0, 1)]
        late_t = reorder(t_factors[2], by_z)
        vectors = apply_pair(late, early, late_t, early_t, vectors, row_size)

        both = jnp.concatenate([own[:2], other[:2]], 1)
        panels = gather(behind(both, near), along_x_and_core(col_size))
        late_t, early_t = reorder(t_factors[0], by_z), reorder(t_factors[1], by_z)
        return apply_pair(((panels, 0),), ((panels, 1),), late_t, early_t, vectors, row_size)

    in_specs = (P(("row", "col"), None), P(None, "row", "col"), P())
    return jax.shard_map(local, mesh=mesh, in_specs=in_specs, out_specs=P("row", "col"), check_vma=False)
```

```python
import functools

import jax
import jax.numpy as jnp
from jax import lax
from jax.experimental import pallas as pl
from jax.experimental.pallas import tpu as pltpu
from jax.sharding import PartitionSpec as P

HIGHEST = lax.Precision.HIGHEST
TILE = 1024
DEPTH = 4
VMEM = 50 * 2**20

X_SIZE = 4


def split(values):
    high = values.astype(jnp.bfloat16)
    return high, (values - high.astype(jnp.float32)).astype(jnp.bfloat16)


def three_pass(left, right, dims):
    mul = functools.partial(
        lax.dot_general, dimension_numbers=(dims, ((), ())), preferred_element_type=jnp.float32
    )
    return mul(left[0], right[0]) + (mul(left[0], right[1]) + mul(left[1], right[0]))


def read(refs):
    return jnp.concatenate([ref[...] for ref in refs], 0)


def panel_specs(parts):
    return [buffered((part.shape[0], TILE), lambda i: (0, i)) for part in parts]


def buffered(shape, index):
    return pl.BlockSpec(shape, index, pipeline_mode=pl.Buffered(DEPTH))


def views(refs, parts):
    return [ref if index is None else ref.at[index] for ref, (_, index) in zip(refs, parts)]


def arrays(parts):
    return [array for array, _ in parts]


def shapes(parts):
    return tuple((array.shape, index) for array, index in parts)


def height(parts):
    return sum(array.shape[-2] for array, _ in parts)


def sums_kernel(late, early, *refs):
    n_late, n_early = len(late), len(early)
    out_ref = refs[-1]
    panels = views(refs, late + early)
    rows, columns = refs[-2].shape
    out_ref[...] = jnp.zeros_like(out_ref)

    def body(*tiles):
        late, early = split(read(tiles[:n_late])), split(read(tiles[n_late : n_late + n_early]))
        vectors = split(tiles[-1][...])
        size = late[0].shape[0]
        both = tuple(jnp.concatenate([e, l], 0) for e, l in zip(early, late))
        out_ref[0 : 2 * size, :] += three_pass(both, vectors, ((1,), (0,)))
        out_ref[2 * size : 3 * size, :] += three_pass(late, early, ((1,), (1,)))

    pltpu.emit_pipeline(
        body,
        grid=(rows // TILE,),
        in_specs=[*panel_specs(panels), buffered((TILE, columns), lambda i: (i, 0))],
    )(*panels, refs[-2])


def pair_sums(late, early, vectors):
    rows, columns = vectors.shape
    size = height(late)
    anywhere = pl.BlockSpec(memory_space=pl.ANY)
    return pl.pallas_call(
        functools.partial(sums_kernel, shapes(late), shapes(early)),
        in_specs=[anywhere] * (len(late) + len(early) + 1),
        out_specs=pl.BlockSpec(memory_space=pltpu.VMEM),
        out_shape=jax.ShapeDtypeStruct((3 * size, columns), jnp.float32),
        compiler_params=pltpu.CompilerParams(vmem_limit_bytes=VMEM),
        cost_estimate=pl.CostEstimate(
            flops=18 * size * rows * columns,
            bytes_accessed=4 * rows * (2 * size + columns),
            transcendentals=0,
        ),
    )(*arrays(late + early), vectors)


def update_kernel(late, early, *refs):
    n_late, n_early = len(late), len(early)
    count = n_late + n_early
    panels = views(refs, late + early)
    sums_ref, late_t_ref, early_t_ref, vectors_ref, out_ref, high_ref, low_ref = refs[count:]
    rows, columns = vectors_ref.shape
    size = late_t_ref.shape[0]

    def body(*tiles):
        @pl.when(pl.program_id(0) == 0)
        def _():
            early_coeffs = exact(early_t_ref[...], sums_ref[0:size, :])
            rest = sums_ref[size : 2 * size, :] - exact(sums_ref[2 * size : 3 * size, :], early_coeffs)
            high, low = split(jnp.concatenate([early_coeffs, exact(late_t_ref[...], rest)], 0))
            high_ref[...] = high
            low_ref[...] = low

        both = split(read((*tiles[n_late:count], *tiles[:n_late])))
        change = three_pass(both, (high_ref[...], low_ref[...]), ((0,), (0,)))
        tiles[-1][...] = tiles[-2][...] - change

    block = buffered((TILE, columns), lambda i: (i, 0))
    pltpu.emit_pipeline(
        body,
        grid=(rows // TILE,),
        in_specs=[*panel_specs(panels), block],
        out_specs=[pl.BlockSpec((TILE, columns), lambda i: (i, 0))],
    )(*panels, vectors_ref, out_ref)


def pair_update(late, early, sums, late_t, early_t, vectors):
    rows, columns = vectors.shape
    size = height(late)
    anywhere = pl.BlockSpec(memory_space=pl.ANY)
    vmem = pl.BlockSpec(memory_space=pltpu.VMEM)
    return pl.pallas_call(
        functools.partial(update_kernel, shapes(late), shapes(early)),
        in_specs=[*[anywhere] * (len(late) + len(early)), vmem, vmem, vmem, anywhere],
        out_specs=anywhere,
        out_shape=jax.ShapeDtypeStruct((rows, columns), jnp.float32),
        scratch_shapes=[pltpu.VMEM((2 * size, columns), jnp.bfloat16)] * 2,
        compiler_params=pltpu.CompilerParams(vmem_limit_bytes=VMEM),
        cost_estimate=pl.CostEstimate(
            flops=12 * size * rows * columns,
            bytes_accessed=4 * rows * (2 * size + 2 * columns),
            transcendentals=0,
        ),
    )(*arrays(late + early), sums, late_t, early_t, vectors)


def add_kernel(slices_ref, copies_ref):
    copies_ref[...] = jnp.broadcast_to(jnp.sum(slices_ref[...], 0, keepdims=True), copies_ref.shape)


def sum_rows(values, size):
    slices = values.reshape(size, values.shape[0] // size, values.shape[1])
    slices = lax.all_to_all(slices, "row", split_axis=0, concat_axis=0, tiled=True)
    copies = pl.pallas_call(add_kernel, out_shape=jax.ShapeDtypeStruct(slices.shape, slices.dtype))(slices)
    return lax.all_to_all(copies, "row", split_axis=0, concat_axis=0, tiled=True).reshape(values.shape)


def exact(a, b):
    return jnp.matmul(a, b, precision=HIGHEST, preferred_element_type=jnp.float32)


def step(z, x, core, size):
    return [(i, (i // 8 ^ z) * 8 + (i // 2 + x) % X_SIZE * 2 + (i % 2 ^ core)) for i in range(size)]


def send(value, z=0, x=0, core=0):
    return lax.ppermute(value, "col", step(z, x, core, lax.axis_size("col")))


def gather(value, groups):
    return lax.all_gather(value, "col", axis=value.ndim - 2, tiled=True, axis_index_groups=groups)


def along_x_and_core(size):
    return [[z * 8 + rest for rest in range(8)] for z in range(size // 8)]


def behind(value, first):
    return lax.optimization_barrier((value, first))[0]


def reorder(factor, places):
    z, x, core = (jnp.stack([jnp.asarray(place[axis]) for place in places]) for axis in range(3))
    width = factor.shape[0] // len(places)
    column = (z % 2 * 8 + x % X_SIZE * 2 + core % 2)[:, None] * width + jnp.arange(width)[None]
    pick = (column.reshape(-1, 1) == jnp.arange(factor.shape[0])[None]).astype(jnp.float32)
    return exact(exact(pick, factor), pick.T)


def apply_pair(late, early, late_t, early_t, vectors, row_size):
    sums = sum_rows(pair_sums(late, early, vectors), row_size)
    return pair_update(late, early, sums, late_t, early_t, vectors)


def solution(mesh):
    row_size, col_size = mesh.shape["row"], mesh.shape["col"]
    cat = functools.partial(jnp.concatenate, axis=0)

    def local(band_vectors, reflectors, t_factors):
        rows, width = reflectors.shape[1:]
        own = jnp.swapaxes(reflectors, 1, 2)
        me = lax.axis_index("col")
        z, x, core = me // 8, me // 2 % X_SIZE, me % 2

        near = gather(own[3], along_x_and_core(col_size))
        blocks = band_vectors.reshape(rows // col_size, col_size, -1).transpose(1, 0, 2)
        vectors = lax.all_to_all(blocks, "col", split_axis=0, concat_axis=0, tiled=True)
        vectors = vectors.reshape(rows, -1)
        other = behind(send(own[:3], z=1), blocks)

        blocks_x = near.reshape(X_SIZE, 2, width, rows)
        far = send(lax.dynamic_index_in_dim(blocks_x, core, 1, False).reshape(-1, rows), z=1)
        early = ((near, None), (far, None), (send(far, core=1), None))
        early_t = reorder(
            t_factors[3],
            [(z, i, c) for i in range(X_SIZE) for c in (0, 1)]
            + [(z + 1, i, core + dc) for dc in (0, 1) for i in range(X_SIZE)],
        )
        late = ((gather(behind(cat([own[2], other[2]]), near), along_x_and_core(col_size)), None),)
        by_z = [(z + dz, i, c) for i in range(X_SIZE) for c in (0, 1) for dz in (0, 1)]
        late_t = reorder(t_factors[2], by_z)
        vectors = apply_pair(late, early, late_t, early_t, vectors, row_size)

        both = jnp.concatenate([own[:2], other[:2]], 1)
        panels = gather(behind(both, near), along_x_and_core(col_size))
        late_t, early_t = reorder(t_factors[0], by_z), reorder(t_factors[1], by_z)
        return apply_pair(((panels, 0),), ((panels, 1),), late_t, early_t, vectors, row_size)

    in_specs = (P(("row", "col"), None), P(None, "row", "col"), P())
    return jax.shard_map(local, mesh=mesh, in_specs=in_specs, out_specs=P("row", "col"), check_vma=False)
```
